32 devices in a mesh: groups: 2 (over y), ep: 4 (over z), tp: 4 (over x, core).
Axes of the slice: x: 2, y: 2, z: 4, core: 2. Of those that a mesh axis runs over, the one named last changes fastest.
Arguments:
- normed: bfloat16 [32, 4096], P(('groups', 'ep'), 'tp'), parts along dimension 0, may hold values from -6 to 6
- residual: bfloat16 [32, 4096], P(('groups', 'ep'), 'tp'), parts along dimension 0, may hold values from -4 to 4
- expert_ids: int32 [32, 2], P(('groups', 'ep')), parts along dimension 0, may hold values from 0 to 3, all different within a row; in each aligned block of 4 rows (0 to 3, 4 to 7, ...) at most 3 rows name the same one
- route_weight: float32 [32, 2], P(('groups', 'ep')), parts along dimension 0, may hold values from 0.05 to 1
- w_gate: bfloat16 [4, 4096, 1024], P('ep', 'tp'), may hold values from -0.09375 to 0.09375
- w_up: bfloat16 [4, 4096, 1024], P('ep', 'tp'), may hold values from -0.09375 to 0.09375
- w_down: bfloat16 [4, 1024, 4096], P('ep', None, 'tp'), may hold values from -0.1875 to 0.1875
- w_kv: bfloat16 [4096, 1024], P('tp'), may hold values from -0.09375 to 0.09375
- key_gain: float32 [128], replicated, may hold values from 0.1 to 1.9
- prefill_kv: bfloat16 [8, 4, 80, 1024], P(('groups', 'ep'), None, None, 'tp'), parts along dimension 0
- order: int32 [8, 4], P(('groups', 'ep')), parts along dimension 0, may hold values from 0 to 3, each once within a row
- lengths: int32 [32], P(('groups', 'ep', 'tp')), parts along dimension 0, may hold values from 2 to 80
- queries: bfloat16 [32, 8192], P(('groups', 'ep', 'tp')), parts along dimension 0
Outputs:
- hidden_state: bfloat16 [32, 4096], P(('groups', 'ep'), 'tp'), parts along dimension 0
- attention: bfloat16 [32, 8192], P(('groups', 'ep', 'tp')), parts along dimension 0
The draws below stay inside these ranges and needn't reach their ends.
There are 2 independent parts, one for each index of `groups`. The reference program is written for one: setup_inputs(seed, part) draws one part's arguments, and reference() takes and returns one part's arrays. A program takes and returns all parts, laid end to end along the dimension named above; an argument that names none is the same for every part. Nothing has to cross between parts.
Inputs may be any that keep to these rules, and one draw needn't show every extreme that they name: `expert_ids`: in the rows of one decode rank (aligned blocks of 4 rows), no expert is named by more than 3 rows; some expert is named by exactly 3 of them in some blocks. Each row names 2 different experts. `order`: each row is a permutation of 0 to 3.
All inputs are finite; a program needn't handle non-finite values.
Results may differ from the reference program's by a relative error of at most 0.0053.
Values may be sent and summed in bfloat16 or wider, within the bound.
A program may use at most 64 MiB of HBM per device.

```python
import math
import jax
import jax.numpy as jnp
import numpy as np
from jax import lax

D = 4096
QH = 64
KVH = 4
HD = 128
FF = 1024
CTX = 80
EXPERTS = 4
TOPK = 2
PRE = 4
ROWS_EP = 4
TOKENS = 16
CAP = 3
KVF = 1024
N_EP = 4


def draw_prefill_kv(key, part):
    key = jax.random.fold_in(key, 11)
    shape = (N_EP, PRE, CTX, KVF)
    base = jax.random.normal(key, shape, jnp.float32)
    return base.astype(jnp.bfloat16)


def draw_queries(key, part):
    key = jax.random.fold_in(key, 23)
    shape = (TOKENS, QH * HD)
    base = jax.random.normal(key, shape, jnp.float32)
    return base.astype(jnp.bfloat16)


def set_ends(drawn, stream_key, smallest, high):
    dims = drawn.shape
    index_at = [jax.random.randint(jax.random.fold_in(stream_key, axis), (), 0, dims[axis]) for axis in range(len(dims))]
    drawn = drawn.at[tuple(index_at)].set(smallest)
    longest = dims.index(max(dims))
    index_at[longest] = (index_at[longest] + 1) % dims[longest]
    return drawn.at[tuple(index_at)].set(high)


def block_scale(key, extent, cuts, least, largest):
    def one(position, blocks):
        draws = jax.random.uniform(jax.random.fold_in(jax.random.fold_in(key, 6), position), (blocks,), jnp.float32, least / len(cuts), largest / len(cuts))
        return jnp.repeat(jnp.exp(draws), extent[position] // blocks).reshape((-1,) + (1,) * (len(extent) - position - 1))

    gain = one(*cuts[0])
    for cut in cuts[1:]:
        gain = gain * one(*cut)
    return gain


def routed_block(stream_key, own, number, rows, number_of, top, most, skew):
    ranking = jax.random.permutation(stream_key, number_of)
    crowded, common = shares(number_of, rows * top, most, skew, True), shares(number_of, rows * top, most, skew, False)
    places = jnp.arange(number_of)

    def named(tallies, rotation):
        used = int((tallies > 0).sum())
        fixed = max(1, used // 4)
        passed = fixed + (places - fixed + rotation * (used - fixed)) % max(1, number_of - fixed)
        return jnp.zeros((number_of,), jnp.int32).at[ranking[jnp.where(places < fixed, places, passed)]].set(jnp.asarray(tallies, jnp.int32))

    tallies = jnp.where(number % 4 == 0, named(crowded, number // 4), named(common, number - number // 4 - 1))
    mixed = jax.random.permutation(jax.random.fold_in(own, 3), number_of)
    donor, receiver = mixed[0:number_of // 2 * 2:2], mixed[1:number_of // 2 * 2:2]
    margin = jnp.minimum(tallies[donor] - 1, most - tallies[receiver]) // 2
    margin = jnp.where((donor == ranking[0]) | (receiver == ranking[0]) | (tallies[receiver] == 0), 0, jnp.maximum(margin, 0))
    passed = jax.random.randint(jax.random.fold_in(own, 4), (number_of // 2,), 0, 1 << 20) % (margin + 1)
    tallies = tallies.at[donor].add(-passed).at[receiver].add(passed)
    members = jnp.searchsorted(jnp.cumsum(tallies), jnp.arange(rows * top), side="right").astype(jnp.int32)
    listing = members.reshape(top, rows).T
    listing = listing[jax.random.permutation(jax.random.fold_in(own, 1), rows)]
    rotation = jax.random.randint(jax.random.fold_in(own, 2), (rows, 1), 0, top)
    return jnp.take_along_axis(listing, (jnp.arange(top)[None, :] + rotation) % top, axis=1)


def shares(amount, total, most, skew, full):
    loads = [(1 << 20) // math.isqrt(rank ** skew) + 1 for rank in range(1, amount + 1)]
    largest = most if full else min(most, max(-(-total // amount), total * loads[0] // sum(loads)))
    least = 1 if total - largest >= amount - 1 else 0
    counts, rest = [largest] + [least] * (amount - 1), total - largest - least * (amount - 1)
    while rest > 0:
        candidates = [i for i in range(1, amount) if counts[i] < largest] or [i for i in range(1, amount) if counts[i] < most]
        whole, left = sum([loads[i] for i in candidates]), rest
        for i in candidates:
            more = min(most - counts[i], max(1, left * loads[i] // whole), rest)
            counts[i] = counts[i] + more
            rest = rest - more
    return np.array(counts)


def gaussian(stream_key, dims, deviation, bound, shards=(), kind=jnp.bfloat16):
    drawn = deviation * jax.random.normal(stream_key, dims, jnp.float32)
    if shards:
        drawn = drawn * block_scale(stream_key, dims, shards, -0.22, 0.18)
    return jnp.clip(drawn, -bound, bound).astype(kind)


def setup_inputs(seed: int = 0, part: int = 0) -> dict:
    key_list = jax.random.split(jax.random.key(seed), 14)
    part_splits = jax.random.split(jax.random.fold_in(key_list[13], part), 14)
    normed = gaussian(part_splits[0], (TOKENS, D), 1.0, 6.0, ((0, 4), (1, 4)))
    residual = gaussian(part_splits[1], (TOKENS, D), 0.5, 4.0, ((0, 4), (1, 4)))
    expert_ids_keys = jax.random.split(jax.random.fold_in(part_splits[2], 1), TOKENS // ROWS_EP)
    expert_ids_turns = jax.random.permutation(jax.random.fold_in(part_splits[2], 3), TOKENS // ROWS_EP)
    expert_ids = jax.vmap(lambda own, number: routed_block(jax.random.fold_in(part_splits[2], 2), own, number, ROWS_EP, EXPERTS, TOPK, CAP, 2))(expert_ids_keys, expert_ids_turns).reshape((TOKENS, TOPK))
    route_weight = jnp.clip(jnp.exp(math.log(1.0) - 2.9957323 * jax.random.uniform(part_splits[3], (TOKENS, TOPK), jnp.float32) ** block_scale(part_splits[3], (TOKENS, TOPK), ((0, 4),), -0.2, 0.2)), 0.05, 1.0)
    w_gate = gaussian(key_list[4], (EXPERTS, D, FF), D ** -0.5, 0.09375, ((0, 4), (1, 4)))
    w_up = gaussian(key_list[5], (EXPERTS, D, FF), D ** -0.5, 0.09375, ((0, 4), (1, 4)))
    w_down = gaussian(key_list[6], (EXPERTS, FF, D), FF ** -0.5, 0.1875, ((0, 4), (2, 4)))
    w_kv = gaussian(key_list[7], (D, KVF), D ** -0.5, 0.09375, ((0, 4),))
    key_gain = jnp.clip(1.0 + 0.18 * jax.random.normal(key_list[8], (HD,), jnp.float32), 0.1, 1.9)
    prefill_kv = draw_prefill_kv(jax.random.fold_in(jax.random.fold_in(key_list[13], part), 71), part)
    order = jax.vmap(lambda own: jax.random.permutation(own, PRE))(jax.random.split(part_splits[10], N_EP)).reshape((N_EP, PRE)).astype(jnp.int32)
    lengths = set_ends(jax.random.randint(part_splits[11], (TOKENS,), 2, CTX + 1), jax.random.fold_in(part_splits[11], 1), 2, CTX).astype(jnp.int32)
    queries = draw_queries(jax.random.fold_in(jax.random.fold_in(key_list[13], part), 71), part)
    return {"normed": normed, "residual": residual, "expert_ids": expert_ids, "route_weight": route_weight, "w_gate": w_gate, "w_up": w_up, "w_down": w_down, "w_kv": w_kv, "key_gain": key_gain, "prefill_kv": prefill_kv, "order": order, "lengths": lengths, "queries": queries}


def rotary_key(key_rows, positions):
    half_size = HD // 2
    exponent = jnp.arange(half_size, dtype=jnp.float32) * (-2.0 / HD)
    frequency = jnp.power(jnp.float32(1000000.0), exponent)
    angles = positions.astype(jnp.float32)[:, None, None] * frequency[None, None, :]
    cosine = jnp.cos(angles)
    sine_part = jnp.sin(angles)
    leading = key_rows[..., :half_size]
    trailing = key_rows[..., half_size:]
    return jnp.concatenate([leading * cosine - trailing * sine_part, trailing * cosine + leading * sine_part], axis=-1)

def attend(query_rows, cache, fresh, lengths, key_gain):
    rows = query_rows.shape[0]
    ctx = cache.shape[1]
    inv_root = 1.0 / jnp.sqrt(jnp.float32(HD))
    parts = fresh.reshape(rows, KVH, 2, HD)
    new_key = parts[:, :, 0].astype(jnp.float32)
    factor = lax.rsqrt(lax.optimization_barrier(jnp.mean(new_key * new_key, axis=-1, keepdims=True)) + 1e-06)
    new_key = rotary_key(new_key * factor * key_gain, lengths).astype(jnp.bfloat16)
    new_value = parts[:, :, 1]
    stored = cache.reshape(rows, ctx, KVH, 2, HD)
    keys = stored[:, :, :, 0].astype(jnp.float32)
    values = stored[:, :, :, 1].astype(jnp.float32)
    query = query_rows.reshape(rows, KVH, QH // KVH, HD).astype(jnp.float32)
    scores = jnp.einsum('rgqd,rcgd->rgqc', query, keys) * inv_root
    fresh_score = jnp.einsum('rgqd,rgd->rgq', query, new_key.astype(jnp.float32)) * inv_root
    live = (jnp.arange(ctx, dtype=jnp.int32)[None, :] < lengths[:, None])[:, None, None, :]
    scores = jnp.where(live, scores, jnp.float32(-1e+30))
    top = jnp.maximum(lax.optimization_barrier(jnp.max(scores, axis=-1)), fresh_score)
    weights = jnp.where(live, jnp.exp(scores - top[..., None]), jnp.float32(0.0))
    fresh_weight = jnp.exp(fresh_score - top)
    total = lax.optimization_barrier(jnp.sum(weights, axis=-1)) + fresh_weight
    probs = (weights / total[..., None]).astype(jnp.bfloat16).astype(jnp.float32)
    fresh_prob = (fresh_weight / total).astype(jnp.bfloat16).astype(jnp.float32)
    out = jnp.einsum('rgqc,rcgd->rgqd', probs, values)
    out = out + fresh_prob[..., None] * new_value.astype(jnp.float32)[:, :, None, :]
    return out.reshape(rows, QH * HD).astype(jnp.bfloat16)

def reference(normed, residual, expert_ids, route_weight, w_gate, w_up, w_down, w_kv, key_gain, prefill_kv, order, lengths, queries):
    share = route_weight / lax.optimization_barrier(jnp.sum(route_weight, axis=1, keepdims=True))
    slots = N_EP * CAP

    def expert_term(carry, expert):
        hit = expert_ids == expert
        live = jnp.any(hit, axis=1)
        picked = jnp.nonzero(live, size=slots, fill_value=0)[0].astype(jnp.int32)
        valid = (jnp.arange(slots, dtype=jnp.int32) < jnp.sum(live.astype(jnp.int32))).astype(jnp.float32)
        rows = normed[picked]
        gate = jnp.dot(rows, w_gate[expert], preferred_element_type=jnp.float32)
        up = jnp.dot(rows, w_up[expert], preferred_element_type=jnp.float32)
        inner = (jax.nn.silu(gate) * up).astype(jnp.bfloat16)
        result = jnp.dot(inner, w_down[expert], preferred_element_type=jnp.float32).astype(jnp.bfloat16)
        weight = lax.optimization_barrier(jnp.sum(jnp.where(hit[picked], share[picked], jnp.float32(0.0)), axis=1)) * valid
        carry = carry.at[picked].add(weight[:, None] * result.astype(jnp.float32))
        return (carry, None)
    mixed, _ = lax.scan(expert_term, jnp.zeros((TOKENS, D), jnp.float32), jnp.arange(EXPERTS, dtype=jnp.int32))
    hidden_state = (residual.astype(jnp.float32) + mixed).astype(jnp.bfloat16)
    fresh = jnp.dot(hidden_state, w_kv, preferred_element_type=jnp.float32).astype(jnp.bfloat16)
    arranged = jnp.take_along_axis(prefill_kv, order[:, :, None, None], axis=1)
    cache = arranged.reshape(N_EP, N_EP, PRE // N_EP, CTX, KVF).transpose(1, 0, 2, 3, 4).reshape(TOKENS, CTX, KVF)
    attention = attend(queries, cache, fresh, lengths, key_gain)
    return (hidden_state, attention)
```

```python
import functools
import math

import jax
import jax.numpy as jnp
from jax import lax
from jax.experimental import pallas as pl
from jax.experimental.pallas import tpu as pltpu
from jax.sharding import PartitionSpec as P

KVH = 4
HD = 128
MESH = pl.DeviceIdType.MESH
F32 = jnp.float32
BF16 = jnp.bfloat16


def flip(index, mask):
    out = index
    bit = 1
    while bit <= mask:
        if mask & bit:
            out = out + bit - 2 * bit * ((index // bit) % 2)
        bit *= 2
    return out


def kernel(
    N, T, R, M, PJ, CTX, KF, FS,
    x_hbm, res_hbm, ids_ref, rw_ref, wg_hbm, wu_hbm, wd_hbm, wkv_hbm, gain_ref,
    kv_hbm, order_ref, len_ref, q_hbm,
    hid_ref, att_ref,
    xbuf, xs, wg_v, wu_v, wd_v, wkv_v, res_v, q_v, qs, kv_v, abuf, cbuf,
    sbuf, rbuf, ibuf, rs, obuf, ebuf, fs, fbuf, frecv,
    lsem, wsem, xs_s, xs_r, c_s, c_r, g_s, g_r, i_s, i_r, e_s, e_r, f_s, f_r,
):
    group = lax.axis_index("groups")
    me = lax.axis_index("ep")
    mt = lax.axis_index("tp")
    QG = qs.shape[1] // KVH

    def dev(e, t):
        return (group, e, t)

    def remote(src, dst, ssem, rsem, e, t):
        return pltpu.make_async_remote_copy(
            src_ref=src, dst_ref=dst, send_sem=ssem, recv_sem=rsem,
            device_id=dev(e, t), device_id_type=MESH,
        )

    peers = [flip(mt, T - 1 - k) for k in range(T)]
    nexts = [lax.rem(me + j, N) for j in range(N)]

    load_kv = pltpu.make_async_copy(kv_hbm.at[0], kv_v, lsem.at[0])
    load_kv.start()
    load_x = pltpu.make_async_copy(x_hbm, xbuf.at[0], lsem.at[1])
    load_x.start()
    load_w = []
    for k in range(T):
        cols = pl.ds(pl.multiple_of(peers[k] * FS, FS), FS)
        a = pltpu.make_async_copy(wg_hbm.at[0, :, cols], wg_v.at[k], wsem.at[0, k])
        b = pltpu.make_async_copy(wu_hbm.at[0, :, cols], wu_v.at[k], wsem.at[1, k])
        a.start()
        b.start()
        load_w.append((a, b))
    load_q = pltpu.make_async_copy(q_hbm, q_v, lsem.at[2])
    load_q.start()
    load_d = pltpu.make_async_copy(wd_hbm.at[0], wd_v, lsem.at[3])
    load_d.start()
    load_r = pltpu.make_async_copy(res_hbm, res_v, lsem.at[4])
    load_r.start()
    load_k = pltpu.make_async_copy(wkv_hbm, wkv_v, lsem.at[5])
    load_k.start()

    barrier = pltpu.get_barrier_semaphore()
    for j in range(1, N):
        pl.semaphore_signal(barrier, inc=1, device_id=dev(nexts[j], mt), device_id_type=MESH)
    for k in range(T - 1):
        pl.semaphore_signal(barrier, inc=1, device_id=dev(me, peers[k]), device_id_type=MESH)
    expected = N - 1 + T - 1
    for m in range(M):
        p = (mt * M + m) // PJ
        for t in range(T):
            @pl.when(jnp.logical_not((p == me) & (mt == t)))
            def _():
                pl.semaphore_signal(barrier, inc=1, device_id=dev(p, t), device_id_type=MESH)
    for j in range(PJ):
        expected = expected + N - jnp.where((me * PJ + j) // M == mt, 1, 0)

    load_kv.wait()
    for i in range(N * PJ):
        abuf[i] = kv_v[order_ref[0, i]]
    load_x.wait()
    pl.semaphore_wait(barrier, expected)

    dispatch = []
    for j in range(1, N):
        c = remote(xbuf.at[0], xbuf.at[j], xs_s.at[j], xs_r.at[j], nexts[j], mt)
        c.start()
        dispatch.append(c)

    def cache_copy(d, j):
        place = me * PJ + j
        t = place // M
        m = place % M
        i = d * PJ + j
        return (d == me) & (t == mt), m, remote(
            abuf.at[i], cbuf.at[mt, m], c_s.at[i], c_r.at[mt, m], d, t
        )

    for d in range(N):
        for j in range(PJ):
            own, m, c = cache_copy(d, j)

            @pl.when(own)
            def _():
                cbuf[mt, m] = abuf[d * PJ + j]

            @pl.when(jnp.logical_not(own))
            def _():
                c.start()

    load_q.wait()
    for m in range(M):
        for h in range(qs.shape[1]):
            qs[m, h : h + 1, :] = q_v[m : m + 1, h * HD : (h + 1) * HD].astype(F32)
    lane = lax.broadcasted_iota(jnp.int32, (1, HD), 1)
    half = jnp.where(lane < HD // 2, lane, lane - HD // 2).astype(F32)
    frequency = jnp.exp(half * F32(-2.0 / HD * math.log(1000000.0)))
    turns = []
    for m in range(M):
        angle = len_ref[m].astype(F32) * frequency
        sine = jnp.sin(angle)
        turns.append((jnp.cos(angle), jnp.where(lane < HD // 2, -sine, sine)))

    for c in dispatch:
        c.wait_recv()
    for e in range(N):
        slot = lax.rem(me - e + N, N)
        xs[e * R : (e + 1) * R, :] = xbuf[slot].astype(F32)
    x = xs[...].astype(BF16)

    scatter = []
    for k in range(T):
        load_w[k][0].wait()
        gate = jnp.dot(x, wg_v[k], preferred_element_type=F32)
        load_w[k][1].wait()
        up = jnp.dot(x, wu_v[k], preferred_element_type=F32)
        if k < T - 1:
            sbuf[k, :, :FS] = gate.astype(BF16)
            sbuf[k, :, FS:] = up.astype(BF16)
            c = remote(sbuf.at[k], rbuf.at[k], g_s.at[k], g_r.at[k], me, peers[k])
            c.start()
            scatter.append(c)
    for k in range(T - 2, -1, -1):
        scatter[k].wait_recv()
        gate = gate + rbuf[k, :, :FS].astype(F32)
        up = up + rbuf[k, :, FS:].astype(F32)
    ibuf[T - 1] = (gate / (1.0 + jnp.exp(-gate)) * up).astype(BF16)
    gather = []
    for k in range(T - 1):
        c = remote(ibuf.at[T - 1], ibuf.at[k], i_s.at[k], i_r.at[k], me, peers[k])
        c.start()
        gather.append(c)

    load_d.wait()

    def down(k):
        rows = pl.ds(pl.multiple_of(peers[k] * FS, FS), FS)
        return jnp.dot(ibuf[k], wd_v[rows, :], preferred_element_type=F32)

    total = down(T - 1)
    for k in range(T - 2, -1, -1):
        gather[k].wait_recv()
        total = total + down(k)
    rs[...] = total
    for d in range(N):
        obuf[d] = rs[d * R : (d + 1) * R, :].astype(BF16)
    back = []
    for j in range(1, N):
        c = remote(obuf.at[nexts[j]], ebuf.at[j], e_s.at[j], e_r.at[j], nexts[j], mt)
        c.start()
        back.append(c)

    scale = F32(1.0 / math.sqrt(HD))
    parts = []
    for m in range(M):
        p = (mt * M + m) // PJ
        for t in range(T):
            @pl.when(jnp.logical_not((p == me) & (mt == t)))
            def _():
                remote(abuf.at[0], cbuf.at[t, m], c_s.at[0], c_r.at[t, m], p, t).wait_recv()
        live = lax.broadcasted_iota(jnp.int32, (QG, CTX), 1) < len_ref[m]
        for g in range(KVH):
            at = g * 2 * HD
            keys = cbuf[at // KF, m, :, at % KF : at % KF + HD]
            at = at + HD
            values = cbuf[at // KF, m, :, at % KF : at % KF + HD]
            query = qs[m, g * QG : (g + 1) * QG, :]
            scores = lax.dot_general(
                query.astype(BF16), keys, (((1,), (1,)), ((), ())), preferred_element_type=F32
            ) * scale
            scores = jnp.where(live, scores, F32(-1e30))
            top = jnp.max(scores, axis=1, keepdims=True)
            weights = jnp.where(live, jnp.exp(scores - top), F32(0.0))
            parts.append((
                query, top, jnp.sum(weights, axis=1, keepdims=True),
                jnp.dot(weights.astype(BF16), values, preferred_element_type=F32),
            ))

    share = rw_ref[...] / jnp.sum(rw_ref[...], axis=1, keepdims=True)
    load_r.wait()
    mixed = res_v[...].astype(F32)
    for j in range(N):
        if j:
            back[j - 1].wait_recv()
        e = lax.rem(me - j + N, N)
        weight = jnp.sum(jnp.where(ids_ref[...] == e, share, F32(0.0)), axis=1, keepdims=True)
        block = ebuf[j] if j else obuf[me]
        mixed = mixed + weight * block.astype(F32)
    hidden = mixed.astype(BF16)
    hid_ref[...] = hidden
    load_k.wait()
    fs[...] = jnp.dot(hidden, wkv_v[...], preferred_element_type=F32)
    for t in range(T):
        fbuf[t] = fs[t * M : (t + 1) * M, :]
    sums = []
    for k in range(T - 1):
        c = remote(fbuf.at[peers[k]], frecv.at[k], f_s.at[k], f_r.at[k], me, peers[k])
        c.start()
        sums.append(c)
    fresh = fbuf[mt]
    for k in range(T - 2, -1, -1):
        sums[k].wait_recv()
        fresh = fresh + frecv[k]
    fresh = fresh.astype(BF16).astype(F32)

    for m in range(M):
        cosine, sine = turns[m]
        for g in range(KVH):
            at = g * 2 * HD
            key = fresh[m : m + 1, at : at + HD]
            value = fresh[m : m + 1, at + HD : at + 2 * HD]
            factor = lax.rsqrt(jnp.mean(key * key, axis=1, keepdims=True) + F32(1e-6))
            key = key * factor * gain_ref[...]
            key = (key * cosine + pltpu.roll(key, HD // 2, 1) * sine).astype(BF16).astype(F32)
            query, top, weight, summed = parts[m * KVH + g]
            score = jnp.sum(query * key, axis=1, keepdims=True) * scale
            most = jnp.maximum(top, score)
            old = jnp.exp(top - most)
            new = jnp.exp(score - most)
            out = (summed * old + new * value) / (weight * old + new)
            att_ref[m, g * QG : (g + 1) * QG, :] = out.astype(BF16)

    for c in dispatch + scatter + gather + back + sums:
        c.wait_send()
    for d in range(N):
        for j in range(PJ):
            own, m, c = cache_copy(d, j)

            @pl.when(jnp.logical_not(own))
            def _():
                c.wait_send()


def on_device(
    normed, residual, expert_ids, route_weight, w_gate, w_up, w_down, w_kv,
    key_gain, prefill_kv, order, lengths, queries,
):
    N = lax.axis_size("ep")
    T = lax.axis_size("tp")
    R, W = normed.shape
    M = lengths.shape[0]
    _, requests, CTX, KF = prefill_kv.shape
    PJ = requests // N
    FF = w_gate.shape[2]
    FS = FF // T
    KVF = w_kv.shape[1]
    heads = queries.shape[1] // HD
    rows = N * R
    dma = pltpu.SemaphoreType.DMA
    anywhere = pl.BlockSpec(memory_space=pl.ANY)
    vmem = pl.BlockSpec(memory_space=pltpu.VMEM)
    smem = pl.BlockSpec(memory_space=pltpu.SMEM)
    hidden_state, attention = pl.pallas_call(
        functools.partial(kernel, N, T, R, M, PJ, CTX, KF, FS),
        out_shape=(
            jax.ShapeDtypeStruct((R, W), BF16),
            jax.ShapeDtypeStruct((M, heads, HD), BF16),
        ),
        in_specs=[
            anywhere, anywhere, vmem, vmem, anywhere, anywhere, anywhere, anywhere, vmem,
            anywhere, smem, smem, anywhere,
        ],
        out_specs=(vmem, vmem),
        scratch_shapes=[
            pltpu.VMEM((N, R, W), BF16),
            pltpu.VMEM((rows, W), F32),
            pltpu.VMEM((T, W, FS), BF16),
            pltpu.VMEM((T, W, FS), BF16),
            pltpu.VMEM((FF, W), BF16),
            pltpu.VMEM((W, KVF), BF16),
            pltpu.VMEM((R, W), BF16),
            pltpu.VMEM((M, heads * HD), BF16),
            pltpu.VMEM((M, heads, HD), F32),
            pltpu.VMEM((requests, CTX, KF), BF16),
            pltpu.VMEM((requests, CTX, KF), BF16),
            pltpu.VMEM((T, M, CTX, KF), BF16),
            pltpu.VMEM((T - 1, rows, 2 * FS), BF16),
            pltpu.VMEM((T - 1, rows, 2 * FS), BF16),
            pltpu.VMEM((T, rows, FS), BF16),
            pltpu.VMEM((rows, W), F32),
            pltpu.VMEM((N, R, W), BF16),
            pltpu.VMEM((N, R, W), BF16),
            pltpu.VMEM((R, KVF), F32),
            pltpu.VMEM((T, M, KVF), F32),
            pltpu.VMEM((T - 1, M, KVF), F32),
            dma((6,)), dma((2, T)),
            dma((N,)), dma((N,)),
            dma((requests,)), dma((T, M)),
            dma((T - 1,)), dma((T - 1,)),
            dma((T - 1,)), dma((T - 1,)),
            dma((N,)), dma((N,)),
            dma((T - 1,)), dma((T - 1,)),
        ],
        compiler_params=pltpu.CompilerParams(
            collective_id=0, has_side_effects=True, vmem_limit_bytes=48 * 1024 * 1024
        ),
    )(
        normed, residual, expert_ids, route_weight, w_gate, w_up, w_down, w_kv,
        key_gain.reshape(1, HD), prefill_kv, order, lengths, queries,
    )
    return hidden_state, attention.reshape(M, heads * HD)


def solution(mesh):
    in_specs = (
        P(("groups", "ep"), "tp"),
        P(("groups", "ep"), "tp"),
        P(("groups", "ep"), None),
        P(("groups", "ep"), None),
        P("ep", "tp", None),
        P("ep", "tp", None),
        P("ep", None, "tp"),
        P("tp", None),
        P(),
        P(("groups", "ep"), None, None, "tp"),
        P(("groups", "ep"), None),
        P(("groups", "ep", "tp")),
        P(("groups", "ep", "tp"), None),
    )
    out_specs = (P(("groups", "ep"), "tp"), P(("groups", "ep", "tp"), None))
    return jax.shard_map(
        on_device, mesh=mesh, in_specs=in_specs, out_specs=out_specs, check_vma=False
    )
```

```python
import functools
import math

import jax
import jax.numpy as jnp
from jax import lax
from jax.experimental import pallas as pl
from jax.experimental.pallas import tpu as pltpu
from jax.sharding import PartitionSpec as P

KVH = 4
HD = 128
MESH = pl.DeviceIdType.MESH
F32 = jnp.float32
BF16 = jnp.bfloat16


def flip(index, mask):
    out = index
    bit = 1
    while bit <= mask:
        if mask & bit:
            out = out + bit - 2 * bit * ((index // bit) % 2)
        bit *= 2
    return out


def kernel(
    N, T, R, M, PJ, CTX, KF, FS,
    x_hbm, res_hbm, ids_hbm, rw_hbm, wg_hbm, wu_hbm, wd_hbm, wkv_hbm, gain_hbm,
    kv_hbm, order_hbm, len_hbm, q_hbm,
    hid_ref, att_ref,
    ids_ref, rw_ref, gain_ref, order_ref, len_ref,
    xbuf, xs, wg_v, wu_v, wd_v, wkv_v, res_v, q_v, qs, kv_v, abuf, cbuf,
    sbuf, rbuf, ibuf, rs, obuf, ebuf, fs, fbuf, frecv,
    lsem, wsem, xs_s, xs_r, c_s, c_r, g_s, g_r, i_s, i_r, e_s, e_r, f_s, f_r,
):
    group = lax.axis_index("groups")
    me = lax.axis_index("ep")
    mt = lax.axis_index("tp")
    QG = qs.shape[1] // KVH

    def dev(e, t):
        return (group, e, t)

    def remote(src, dst, ssem, rsem, e, t):
        return pltpu.make_async_remote_copy(
            src_ref=src, dst_ref=dst, send_sem=ssem, recv_sem=rsem,
            device_id=dev(e, t), device_id_type=MESH,
        )

    peers = [flip(mt, T - 1 - k) for k in range(T)]
    nexts = [lax.rem(me + j, N) for j in range(N)]

    load_x = pltpu.make_async_copy(x_hbm, xbuf.at[0], lsem.at[1])
    load_x.start()
    load_o = pltpu.make_async_copy(order_hbm, order_ref, lsem.at[6])
    load_o.start()
    load_kv = pltpu.make_async_copy(kv_hbm.at[0], kv_v, lsem.at[0])
    load_kv.start()
    load_l = pltpu.make_async_copy(len_hbm, len_ref, lsem.at[7])
    load_l.start()
    load_i = pltpu.make_async_copy(ids_hbm, ids_ref, lsem.at[8])
    load_i.start()
    load_s = pltpu.make_async_copy(rw_hbm, rw_ref, lsem.at[9])
    load_s.start()
    load_g = pltpu.make_async_copy(gain_hbm, gain_ref, lsem.at[10])
    load_g.start()
    load_w = []
    for k in range(T):
        cols = pl.ds(pl.multiple_of(peers[k] * FS, FS), FS)
        a = pltpu.make_async_copy(wg_hbm.at[0, :, cols], wg_v.at[k], wsem.at[0, k])
        b = pltpu.make_async_copy(wu_hbm.at[0, :, cols], wu_v.at[k], wsem.at[1, k])
        a.start()
        b.start()
        load_w.append((a, b))
    load_q = pltpu.make_async_copy(q_hbm, q_v, lsem.at[2])
    load_q.start()
    load_d = pltpu.make_async_copy(wd_hbm.at[0], wd_v, lsem.at[3])
    load_d.start()
    load_r = pltpu.make_async_copy(res_hbm, res_v, lsem.at[4])
    load_r.start()
    load_k = pltpu.make_async_copy(wkv_hbm, wkv_v, lsem.at[5])
    load_k.start()

    barrier = pltpu.get_barrier_semaphore()
    for j in range(1, N):
        pl.semaphore_signal(barrier, inc=1, device_id=dev(nexts[j], mt), device_id_type=MESH)
    for k in range(T - 1):
        pl.semaphore_signal(barrier, inc=1, device_id=dev(me, peers[k]), device_id_type=MESH)
    expected = N - 1 + T - 1
    for m in range(M):
        p = (mt * M + m) // PJ
        for t in range(T):
            @pl.when(jnp.logical_not((p == me) & (mt == t)))
            def _():
                pl.semaphore_signal(barrier, inc=1, device_id=dev(p, t), device_id_type=MESH)
    for j in range(PJ):
        expected = expected + N - jnp.where((me * PJ + j) // M == mt, 1, 0)

    load_x.wait()
    pl.semaphore_wait(barrier, expected)

    dispatch = []
    for j in range(1, N):
        c = remote(xbuf.at[0], xbuf.at[j], xs_s.at[j], xs_r.at[j], nexts[j], mt)
        c.start()
        dispatch.append(c)

    def cache_copy(d, j):
        place = me * PJ + j
        t = place // M
        m = place % M
        i = d * PJ + j
        return (d == me) & (t == mt), m, remote(
            abuf.at[i], cbuf.at[mt, m], c_s.at[i], c_r.at[mt, m], d, t
        )

    load_o.wait()
    load_kv.wait()
    for d in range(N):
        for j in range(PJ):
            abuf[d * PJ + j] = kv_v[order_ref[0, d * PJ + j]]
            own, m, c = cache_copy(d, j)

            @pl.when(own)
            def _():
                cbuf[mt, m] = abuf[d * PJ + j]

            @pl.when(jnp.logical_not(own))
            def _():
                c.start()

    load_q.wait()
    load_l.wait()
    load_g.wait()
    for m in range(M):
        for h in range(qs.shape[1]):
            qs[m, h : h + 1, :] = q_v[m : m + 1, h * HD : (h + 1) * HD].astype(F32)
    lane = lax.broadcasted_iota(jnp.int32, (1, HD), 1)
    half = jnp.where(lane < HD // 2, lane, lane - HD // 2).astype(F32)
    frequency = jnp.exp(half * F32(-2.0 / HD * math.log(1000000.0)))
    turns = []
    for m in range(M):
        angle = len_ref[m].astype(F32) * frequency
        sine = jnp.sin(angle)
        turns.append((jnp.cos(angle), jnp.where(lane < HD // 2, -sine, sine)))

    for c in dispatch:
        c.wait_recv()
    for e in range(N):
        slot = lax.rem(me - e + N, N)
        xs[e * R : (e + 1) * R, :] = xbuf[slot].astype(F32)
    x = xs[...].astype(BF16)

    scatter = []
    for k in range(T):
        load_w[k][0].wait()
        gate = jnp.dot(x, wg_v[k], preferred_element_type=F32)
        load_w[k][1].wait()
        up = jnp.dot(x, wu_v[k], preferred_element_type=F32)
        if k < T - 1:
            sbuf[k, :, :FS] = gate.astype(BF16)
            sbuf[k, :, FS:] = up.astype(BF16)
            c = remote(sbuf.at[k], rbuf.at[k], g_s.at[k], g_r.at[k], me, peers[k])
            c.start()
            scatter.append(c)
    for k in range(T - 2, -1, -1):
        scatter[k].wait_recv()
        gate = gate + rbuf[k, :, :FS].astype(F32)
        up = up + rbuf[k, :, FS:].astype(F32)
    ibuf[T - 1] = (gate / (1.0 + jnp.exp(-gate)) * up).astype(BF16)
    gather = []
    for k in range(T - 1):
        c = remote(ibuf.at[T - 1], ibuf.at[k], i_s.at[k], i_r.at[k], me, peers[k])
        c.start()
        gather.append(c)

    load_d.wait()

    def down(k):
        rows = pl.ds(pl.multiple_of(peers[k] * FS, FS), FS)
        return jnp.dot(ibuf[k], wd_v[rows, :], preferred_element_type=F32)

    total = down(T - 1)
    for k in range(T - 2, -1, -1):
        gather[k].wait_recv()
        total = total + down(k)
    rs[...] = total
    for d in range(N):
        obuf[d] = rs[d * R : (d + 1) * R, :].astype(BF16)
    back = []
    for j in range(1, N):
        c = remote(obuf.at[nexts[j]], ebuf.at[j], e_s.at[j], e_r.at[j], nexts[j], mt)
        c.start()
        back.append(c)

    scale = F32(1.0 / math.sqrt(HD))
    parts = []
    for m in range(M):
        p = (mt * M + m) // PJ
        for t in range(T):
            @pl.when(jnp.logical_not((p == me) & (mt == t)))
            def _():
                remote(abuf.at[0], cbuf.at[t, m], c_s.at[0], c_r.at[t, m], p, t).wait_recv()
        live = lax.broadcasted_iota(jnp.int32, (QG, CTX), 1) < len_ref[m]
        for g in range(KVH):
            at = g * 2 * HD
            keys = cbuf[at // KF, m, :, at % KF : at % KF + HD]
            at = at + HD
            values = cbuf[at // KF, m, :, at % KF : at % KF + HD]
            query = qs[m, g * QG : (g + 1) * QG, :]
            scores = lax.dot_general(
                query.astype(BF16), keys, (((1,), (1,)), ((), ())), preferred_element_type=F32
            ) * scale
            scores = jnp.where(live, scores, F32(-1e30))
            top = jnp.max(scores, axis=1, keepdims=True)
            weights = jnp.where(live, jnp.exp(scores - top), F32(0.0))
            parts.append((
                query, top, jnp.sum(weights, axis=1, keepdims=True),
                jnp.dot(weights.astype(BF16), values, preferred_element_type=F32),
            ))

    load_i.wait()
    load_s.wait()
    share = rw_ref[...] / jnp.sum(rw_ref[...], axis=0, keepdims=True)
    diagonal = lax.broadcasted_iota(jnp.int32, (R, R), 0) == lax.broadcasted_iota(
        jnp.int32, (R, R), 1
    )

    def weight_of(e):
        row = jnp.sum(jnp.where(ids_ref[...] == e, share, F32(0.0)), axis=0, keepdims=True)
        return jnp.sum(jnp.where(diagonal, row, F32(0.0)), axis=1, keepdims=True)

    load_r.wait()
    mixed = res_v[...].astype(F32)
    for j in range(N):
        if j:
            back[j - 1].wait_recv()
        e = lax.rem(me - j + N, N)
        block = ebuf[j] if j else obuf[me]
        mixed = mixed + weight_of(e) * block.astype(F32)
    hidden = mixed.astype(BF16)
    hid_ref[...] = hidden
    load_k.wait()
    fs[...] = jnp.dot(hidden, wkv_v[...], preferred_element_type=F32)
    for t in range(T):
        fbuf[t] = fs[t * M : (t + 1) * M, :]
    sums = []
    for k in range(T - 1):
        c = remote(fbuf.at[peers[k]], frecv.at[k], f_s.at[k], f_r.at[k], me, peers[k])
        c.start()
        sums.append(c)
    fresh = fbuf[mt]
    for k in range(T - 2, -1, -1):
        sums[k].wait_recv()
        fresh = fresh + frecv[k]
    fresh = fresh.astype(BF16).astype(F32)

    for m in range(M):
        cosine, sine = turns[m]
        for g in range(KVH):
            at = g * 2 * HD
            key = fresh[m : m + 1, at : at + HD]
            value = fresh[m : m + 1, at + HD : at + 2 * HD]
            factor = lax.rsqrt(jnp.mean(key * key, axis=1, keepdims=True) + F32(1e-6))
            key = key * factor * gain_ref[...]
            key = (key * cosine + pltpu.roll(key, HD // 2, 1) * sine).astype(BF16).astype(F32)
            query, top, weight, summed = parts[m * KVH + g]
            score = jnp.sum(query * key, axis=1, keepdims=True) * scale
            most = jnp.maximum(top, score)
            old = jnp.exp(top - most)
            new = jnp.exp(score - most)
            out = (summed * old + new * value) / (weight * old + new)
            att_ref[m, g * QG : (g + 1) * QG, :] = out.astype(BF16)

    for c in dispatch + scatter + gather + back + sums:
        c.wait_send()
    for d in range(N):
        for j in range(PJ):
            own, m, c = cache_copy(d, j)

            @pl.when(jnp.logical_not(own))
            def _():
                c.wait_send()


def on_device(
    normed, residual, expert_ids, route_weight, w_gate, w_up, w_down, w_kv,
    key_gain, prefill_kv, order, lengths, queries,
):
    N = lax.axis_size("ep")
    T = lax.axis_size("tp")
    R, W = normed.shape
    M = lengths.shape[0]
    _, requests, CTX, KF = prefill_kv.shape
    PJ = requests // N
    FF = w_gate.shape[2]
    FS = FF // T
    KVF = w_kv.shape[1]
    heads = queries.shape[1] // HD
    rows = N * R
    choices = expert_ids.shape[1]
    dma = pltpu.SemaphoreType.DMA
    hbm = pl.BlockSpec(memory_space=pltpu.HBM)
    vmem = pl.BlockSpec(memory_space=pltpu.VMEM)
    hidden_state, attention = pl.pallas_call(
        functools.partial(kernel, N, T, R, M, PJ, CTX, KF, FS),
        out_shape=(
            jax.ShapeDtypeStruct((R, W), BF16),
            jax.ShapeDtypeStruct((M, heads, HD), BF16),
        ),
        in_specs=[hbm] * 13,
        out_specs=(vmem, vmem),
        scratch_shapes=[
            pltpu.VMEM((choices, R), jnp.int32),
            pltpu.VMEM((choices, R), F32),
            pltpu.VMEM((1, HD), F32),
            pltpu.SMEM((1, requests), jnp.int32),
            pltpu.SMEM((M,), jnp.int32),
            pltpu.VMEM((N, R, W), BF16),
            pltpu.VMEM((rows, W), F32),
            pltpu.VMEM((T, W, FS), BF16),
            pltpu.VMEM((T, W, FS), BF16),
            pltpu.VMEM((FF, W), BF16),
            pltpu.VMEM((W, KVF), BF16),
            pltpu.VMEM((R, W), BF16),
            pltpu.VMEM((M, heads * HD), BF16),
            pltpu.VMEM((M, heads, HD), F32),
            pltpu.VMEM((requests, CTX, KF), BF16),
            pltpu.VMEM((requests, CTX, KF), BF16),
            pltpu.VMEM((T, M, CTX, KF), BF16),
            pltpu.VMEM((T - 1, rows, 2 * FS), BF16),
            pltpu.VMEM((T - 1, rows, 2 * FS), BF16),
            pltpu.VMEM((T, rows, FS), BF16),
            pltpu.VMEM((rows, W), F32),
            pltpu.VMEM((N, R, W), BF16),
            pltpu.VMEM((N, R, W), BF16),
            pltpu.VMEM((R, KVF), F32),
            pltpu.VMEM((T, M, KVF), F32),
            pltpu.VMEM((T - 1, M, KVF), F32),
            dma((11,)), dma((2, T)),
            dma((N,)), dma((N,)),
            dma((requests,)), dma((T, M)),
            dma((T - 1,)), dma((T - 1,)),
            dma((T - 1,)), dma((T - 1,)),
            dma((N,)), dma((N,)),
            dma((T - 1,)), dma((T - 1,)),
        ],
        compiler_params=pltpu.CompilerParams(
            collective_id=0, has_side_effects=True, vmem_limit_bytes=64 * 1024 * 1024
        ),
    )(
        normed, residual, expert_ids.T, route_weight.T, w_gate, w_up, w_down, w_kv,
        key_gain.reshape(1, HD), prefill_kv, order, lengths, queries,
    )
    return hidden_state, attention.reshape(M, heads * HD)


def solution(mesh):
    in_specs = (
        P(("groups", "ep"), "tp"),
        P(("groups", "ep"), "tp"),
        P(("groups", "ep"), None),
        P(("groups", "ep"), None),
        P("ep", "tp", None),
        P("ep", "tp", None),
        P("ep", None, "tp"),
        P("tp", None),
        P(),
        P(("groups", "ep"), None, None, "tp"),
        P(("groups", "ep"), None),
        P(("groups", "ep", "tp")),
        P(("groups", "ep", "tp"), None),
    )
    out_specs = (P(("groups", "ep"), "tp"), P(("groups", "ep", "tp"), None))
    return jax.shard_map(
        on_device, mesh=mesh, in_specs=in_specs, out_specs=out_specs, check_vma=False
    )
```

```python
import functools
import math

import jax
import jax.numpy as jnp
from jax import lax
from jax.experimental import pallas as pl
from jax.experimental.pallas import tpu as pltpu
from jax.sharding import PartitionSpec as P

KVH = 4
HD = 128
MESH = pl.DeviceIdType.MESH
F32 = jnp.float32
BF16 = jnp.bfloat16


def flip(index, mask):
    out = index
    bit = 1
    while bit <= mask:
        if mask & bit:
            out = out + bit - 2 * bit * ((index // bit) % 2)
        bit *= 2
    return out


def kernel(
    N, T, R, M, PJ, CTX, KF, FS,
    x_hbm, res_hbm, ids_hbm, rw_hbm, wg_hbm, wu_hbm, wd_hbm, wkv_hbm, gain_hbm,
    kv_hbm, order_hbm, len_hbm, q_hbm,
    hid_ref, att_ref,
    ids_ref, rw_ref, gain_ref, order_ref, len_ref,
    xbuf, xs, wg_v, wu_v, wd_v, wkv_v, res_v, q_v, qs, kv_v, abuf, cbuf,
    sbuf, rbuf, ibuf, rs, obuf, ebuf, wsend, wrecv, ws, rp, ps, pbuf, precv,
    lsem, wsem, xs_s, xs_r, c_s, c_r, g_s, g_r, i_s, i_r, e_s, e_r, w_s, w_r, f_s, f_r,
):
    group = lax.axis_index("groups")
    me = lax.axis_index("ep")
    mt = lax.axis_index("tp")
    QG = qs.shape[1] // KVH

    def dev(e, t):
        return (group, e, t)

    def remote(src, dst, ssem, rsem, e, t):
        return pltpu.make_async_remote_copy(
            src_ref=src, dst_ref=dst, send_sem=ssem, recv_sem=rsem,
            device_id=dev(e, t), device_id_type=MESH,
        )

    peers = [flip(mt, T - 1 - k) for k in range(T)]
    nexts = [lax.rem(me + j, N) for j in range(N)]

    load_x = pltpu.make_async_copy(x_hbm, xbuf.at[0], lsem.at[1])
    load_x.start()
    load_o = pltpu.make_async_copy(order_hbm, order_ref, lsem.at[6])
    load_o.start()
    load_kv = pltpu.make_async_copy(kv_hbm.at[0], kv_v, lsem.at[0])
    load_kv.start()
    load_l = pltpu.make_async_copy(len_hbm, len_ref, lsem.at[7])
    load_l.start()
    load_i = pltpu.make_async_copy(ids_hbm, ids_ref, lsem.at[8])
    load_i.start()
    load_s = pltpu.make_async_copy(rw_hbm, rw_ref, lsem.at[9])
    load_s.start()
    load_g = pltpu.make_async_copy(gain_hbm, gain_ref, lsem.at[10])
    load_g.start()
    load_w = []
    for k in range(T):
        cols = pl.ds(pl.multiple_of(peers[k] * FS, FS), FS)
        a = pltpu.make_async_copy(wg_hbm.at[0, :, cols], wg_v.at[k], wsem.at[0, k])
        b = pltpu.make_async_copy(wu_hbm.at[0, :, cols], wu_v.at[k], wsem.at[1, k])
        a.start()
        b.start()
        load_w.append((a, b))
    load_q = pltpu.make_async_copy(q_hbm, q_v, lsem.at[2])
    load_q.start()
    load_d = pltpu.make_async_copy(wd_hbm.at[0], wd_v, lsem.at[3])
    load_d.start()
    load_r = pltpu.make_async_copy(res_hbm, res_v, lsem.at[4])
    load_r.start()
    load_k = pltpu.make_async_copy(wkv_hbm, wkv_v, lsem.at[5])
    load_k.start()

    barrier = pltpu.get_barrier_semaphore()
    for j in range(N):
        for k in range(T):
            if j or k < T - 1:
                pl.semaphore_signal(
                    barrier, inc=1, device_id=dev(nexts[j], peers[k]), device_id_type=MESH
                )
    load_x.wait()
    pl.semaphore_wait(barrier, N * T - 1)

    dispatch, shares = [], []
    for j in range(1, N):
        c = remote(xbuf.at[0], xbuf.at[j], xs_s.at[j], xs_r.at[j], nexts[j], mt)
        c.start()
        dispatch.append(c)

    load_i.wait()
    load_s.wait()
    share = rw_ref[...] / jnp.sum(rw_ref[...], axis=0, keepdims=True)
    diagonal = lax.broadcasted_iota(jnp.int32, (R, R), 0) == lax.broadcasted_iota(
        jnp.int32, (R, R), 1
    )

    def weight_of(e):
        row = jnp.sum(jnp.where(ids_ref[...] == e, share, F32(0.0)), axis=0, keepdims=True)
        return jnp.sum(jnp.where(diagonal, row, F32(0.0)), axis=1, keepdims=True)

    for e in range(N):
        wsend[e] = jnp.broadcast_to(weight_of(e), (R, HD))
    for j in range(1, N):
        c = remote(wsend.at[nexts[j]], wrecv.at[j], w_s.at[j], w_r.at[j], nexts[j], mt)
        c.start()
        shares.append(c)

    def cache_copy(d, j):
        place = me * PJ + j
        t = place // M
        m = place % M
        i = d * PJ + j
        return (d == me) & (t == mt), m, remote(
            abuf.at[i], cbuf.at[mt, m], c_s.at[i], c_r.at[mt, m], d, t
        )

    load_o.wait()
    load_kv.wait()
    for d in range(N):
        for j in range(PJ):
            abuf[d * PJ + j] = kv_v[order_ref[0, d * PJ + j]]
            own, m, c = cache_copy(d, j)

            @pl.when(own)
            def _():
                cbuf[mt, m] = abuf[d * PJ + j]

            @pl.when(jnp.logical_not(own))
            def _():
                c.start()

    load_q.wait()
    load_l.wait()
    load_g.wait()
    for m in range(M):
        for h in range(qs.shape[1]):
            qs[m, h : h + 1, :] = q_v[m : m + 1, h * HD : (h + 1) * HD].astype(F32)
    lane = lax.broadcasted_iota(jnp.int32, (1, HD), 1)
    half = jnp.where(lane < HD // 2, lane, lane - HD // 2).astype(F32)
    frequency = jnp.exp(half * F32(-2.0 / HD * math.log(1000000.0)))
    turns = []
    for m in range(M):
        angle = len_ref[m].astype(F32) * frequency
        sine = jnp.sin(angle)
        turns.append((jnp.cos(angle), jnp.where(lane < HD // 2, -sine, sine)))

    for c in dispatch:
        c.wait_recv()
    for e in range(N):
        slot = lax.rem(me - e + N, N)
        xs[e * R : (e + 1) * R, :] = xbuf[slot].astype(F32)
    x = xs[...].astype(BF16)

    scatter = []
    for k in range(T):
        load_w[k][0].wait()
        gate = jnp.dot(x, wg_v[k], preferred_element_type=F32)
        load_w[k][1].wait()
        up = jnp.dot(x, wu_v[k], preferred_element_type=F32)
        if k < T - 1:
            sbuf[k, :, :FS] = gate.astype(BF16)
            sbuf[k, :, FS:] = up.astype(BF16)
            c = remote(sbuf.at[k], rbuf.at[k], g_s.at[k], g_r.at[k], me, peers[k])
            c.start()
            scatter.append(c)
    for k in range(T - 2, -1, -1):
        scatter[k].wait_recv()
        gate = gate + rbuf[k, :, :FS].astype(F32)
        up = up + rbuf[k, :, FS:].astype(F32)
    ibuf[T - 1] = (gate / (1.0 + jnp.exp(-gate)) * up).astype(BF16)
    gather = []
    for k in range(T - 1):
        c = remote(ibuf.at[T - 1], ibuf.at[k], i_s.at[k], i_r.at[k], me, peers[k])
        c.start()
        gather.append(c)

    load_r.wait()
    residual = res_v[...].astype(F32)
    for c in shares:
        c.wait_recv()
    for e in range(N):
        rp[e * R : (e + 1) * R, :] = jnp.where(me == e, residual, F32(0.0))
        slot = lax.rem(me - e + N, N)
        ws[e * R : (e + 1) * R, :] = jnp.where(me == e, wsend[me], wrecv[jnp.maximum(slot, 1)])
    load_d.wait()

    def down(k):
        rows = pl.ds(pl.multiple_of(peers[k] * FS, FS), FS)
        return jnp.dot(ibuf[k], wd_v[rows, :], preferred_element_type=F32)

    total = down(T - 1)
    for k in range(T - 2, -1, -1):
        gather[k].wait_recv()
        total = total + down(k)
    total = total.astype(BF16).astype(F32)
    rs[...] = total
    load_k.wait()
    terms = (rp[...] + ws[:, :1] * total).astype(BF16)
    total = jnp.dot(terms, wkv_v[...], preferred_element_type=F32)
    ps[...] = total
    for i in range(N * T):
        pbuf[i] = ps[i * M : (i + 1) * M, :]
    sums = []
    for j in range(N - 1, -1, -1):
        for k in range(T):
            if j or k < T - 1:
                i = j * T + k
                c = remote(
                    pbuf.at[nexts[j] * T + peers[k]], precv.at[i], f_s.at[i], f_r.at[i],
                    nexts[j], peers[k],
                )
                c.start()
                sums.append((i, c))
    for d in range(N):
        obuf[d] = rs[d * R : (d + 1) * R, :].astype(BF16)
    back = []
    for j in range(1, N):
        c = remote(obuf.at[nexts[j]], ebuf.at[j], e_s.at[j], e_r.at[j], nexts[j], mt)
        c.start()
        back.append(c)

    scale = F32(1.0 / math.sqrt(HD))
    parts = []
    for m in range(M):
        p = (mt * M + m) // PJ
        for t in range(T):
            @pl.when(jnp.logical_not((p == me) & (mt == t)))
            def _():
                remote(abuf.at[0], cbuf.at[t, m], c_s.at[0], c_r.at[t, m], p, t).wait_recv()
        live = lax.broadcasted_iota(jnp.int32, (QG, CTX), 1) < len_ref[m]
        for g in range(KVH):
            at = g * 2 * HD
            keys = cbuf[at // KF, m, :, at % KF : at % KF + HD]
            at = at + HD
            values = cbuf[at // KF, m, :, at % KF : at % KF + HD]
            query = qs[m, g * QG : (g + 1) * QG, :]
            scores = lax.dot_general(
                query.astype(BF16), keys, (((1,), (1,)), ((), ())), preferred_element_type=F32
            ) * scale
            scores = jnp.where(live, scores, F32(-1e30))
            top = jnp.max(scores, axis=1, keepdims=True)
            weights = jnp.where(live, jnp.exp(scores - top), F32(0.0))
            parts.append((
                query, top, jnp.sum(weights, axis=1, keepdims=True),
                jnp.dot(weights.astype(BF16), values, preferred_element_type=F32),
            ))

    mixed = res_v[...].astype(F32)
    for j in range(N):
        if j:
            back[j - 1].wait_recv()
        e = lax.rem(me - j + N, N)
        block = ebuf[j] if j else obuf[me]
        mixed = mixed + wsend[e][:, :1] * block.astype(F32)
    hid_ref[...] = mixed.astype(BF16)
    fresh = pbuf[me * T + mt]
    for i, c in sums:
        c.wait_recv()
    for i, c in sums:
        fresh = fresh + precv[i]
    fresh = fresh.astype(BF16).astype(F32)

    for m in range(M):
        cosine, sine = turns[m]
        for g in range(KVH):
            at = g * 2 * HD
            key = fresh[m : m + 1, at : at + HD]
            value = fresh[m : m + 1, at + HD : at + 2 * HD]
            factor = lax.rsqrt(jnp.mean(key * key, axis=1, keepdims=True) + F32(1e-6))
            key = key * factor * gain_ref[...]
            key = (key * cosine + pltpu.roll(key, HD // 2, 1) * sine).astype(BF16).astype(F32)
            query, top, weight, summed = parts[m * KVH + g]
            score = jnp.sum(query * key, axis=1, keepdims=True) * scale
            most = jnp.maximum(top, score)
            old = jnp.exp(top - most)
            new = jnp.exp(score - most)
            out = (summed * old + new * value) / (weight * old + new)
            att_ref[m, g * QG : (g + 1) * QG, :] = out.astype(BF16)

    for c in dispatch + shares + scatter + gather + back + [c for _, c in sums]:
        c.wait_send()
    for d in range(N):
        for j in range(PJ):
            own, m, c = cache_copy(d, j)

            @pl.when(jnp.logical_not(own))
            def _():
                c.wait_send()


def on_device(
    normed, residual, expert_ids, route_weight, w_gate, w_up, w_down, w_kv,
    key_gain, prefill_kv, order, lengths, queries,
):
    N = lax.axis_size("ep")
    T = lax.axis_size("tp")
    R, W = normed.shape
    M = lengths.shape[0]
    _, requests, CTX, KF = prefill_kv.shape
    PJ = requests // N
    FF = w_gate.shape[2]
    FS = FF // T
    KVF = w_kv.shape[1]
    heads = queries.shape[1] // HD
    rows = N * R
    choices = expert_ids.shape[1]
    dma = pltpu.SemaphoreType.DMA
    hbm = pl.BlockSpec(memory_space=pltpu.HBM)
    vmem = pl.BlockSpec(memory_space=pltpu.VMEM)
    hidden_state, attention = pl.pallas_call(
        functools.partial(kernel, N, T, R, M, PJ, CTX, KF, FS),
        out_shape=(
            jax.ShapeDtypeStruct((R, W), BF16),
            jax.ShapeDtypeStruct((M, heads, HD), BF16),
        ),
        in_specs=[hbm] * 13,
        out_specs=(vmem, vmem),
        scratch_shapes=[
            pltpu.VMEM((choices, R), jnp.int32),
            pltpu.VMEM((choices, R), F32),
            pltpu.VMEM((1, HD), F32),
            pltpu.SMEM((1, requests), jnp.int32),
            pltpu.SMEM((M,), jnp.int32),
            pltpu.VMEM((N, R, W), BF16),
            pltpu.VMEM((rows, W), F32),
            pltpu.VMEM((T, W, FS), BF16),
            pltpu.VMEM((T, W, FS), BF16),
            pltpu.VMEM((FF, W), BF16),
            pltpu.VMEM((W, KVF), BF16),
            pltpu.VMEM((R, W), BF16),
            pltpu.VMEM((M, heads * HD), BF16),
            pltpu.VMEM((M, heads, HD), F32),
            pltpu.VMEM((requests, CTX, KF), BF16),
            pltpu.VMEM((requests, CTX, KF), BF16),
            pltpu.VMEM((T, M, CTX, KF), BF16),
            pltpu.VMEM((T - 1, rows, 2 * FS), BF16),
            pltpu.VMEM((T - 1, rows, 2 * FS), BF16),
            pltpu.VMEM((T, rows, FS), BF16),
            pltpu.VMEM((rows, W), F32),
            pltpu.VMEM((N, R, W), BF16),
            pltpu.VMEM((N, R, W), BF16),
            pltpu.VMEM((N, R, HD), F32),
            pltpu.VMEM((N, R, HD), F32),
            pltpu.VMEM((rows, HD), F32),
            pltpu.VMEM((rows, W), F32),
            pltpu.VMEM((rows, KVF), F32),
            pltpu.VMEM((N * T, M, KVF), F32),
            pltpu.VMEM((N * T, M, KVF), F32),
            dma((11,)), dma((2, T)),
            dma((N,)), dma((N,)),
            dma((requests,)), dma((T, M)),
            dma((T - 1,)), dma((T - 1,)),
            dma((T - 1,)), dma((T - 1,)),
            dma((N,)), dma((N,)),
            dma((N,)), dma((N,)),
            dma((N * T,)), dma((N * T,)),
        ],
        compiler_params=pltpu.CompilerParams(
            collective_id=0, has_side_effects=True, vmem_limit_bytes=64 * 1024 * 1024
        ),
    )(
        normed, residual, expert_ids.T, route_weight.T, w_gate, w_up, w_down, w_kv,
        key_gain.reshape(1, HD), prefill_kv, order, lengths, queries,
    )
    return hidden_state, attention.reshape(M, heads * HD)


def solution(mesh):
    in_specs = (
        P(("groups", "ep"), "tp"),
        P(("groups", "ep"), "tp"),
        P(("groups", "ep"), None),
        P(("groups", "ep"), None),
        P("ep", "tp", None),
        P("ep", "tp", None),
        P("ep", None, "tp"),
        P("tp", None),
        P(),
        P(("groups", "ep"), None, None, "tp"),
        P(("groups", "ep"), None),
        P(("groups", "ep", "tp")),
        P(("groups", "ep", "tp"), None),
    )
    out_specs = (P(("groups", "ep"), "tp"), P(("groups", "ep", "tp"), None))
    return jax.shard_map(
        on_device, mesh=mesh, in_specs=in_specs, out_specs=out_specs, check_vma=False
    )
```

```python
import functools
import math

import jax
import jax.numpy as jnp
from jax import lax
from jax.experimental import pallas as pl
from jax.experimental.pallas import tpu as pltpu
from jax.sharding import PartitionSpec as P

KVH = 4
HD = 128
MESH = pl.DeviceIdType.MESH
F32 = jnp.float32
BF16 = jnp.bfloat16


def flip(index, mask):
    out = index
    bit = 1
    while bit <= mask:
        if mask & bit:
            out = out + bit - 2 * bit * ((index // bit) % 2)
        bit *= 2
    return out


def kernel(
    N, T, R, M, PJ, CTX, KF, FS,
    x_hbm, res_hbm, ids_hbm, rw_hbm, wg_hbm, wu_hbm, wd_hbm, wkv_hbm, gain_hbm,
    kv_hbm, order_hbm, len_hbm, q_hbm,
    hid_ref, att_ref,
    ids_ref, rw_ref, gain_ref, order_ref, len_ref,
    xbuf, xs, wg_v, wu_v, wd_v, wkv_v, res_v, q_v, qs, kv_v, abuf, cbuf,
    sbuf, rbuf, ibuf, rs, obuf, ebuf, wsend, wrecv, ws, rp, ps, pbuf, precv,
    lsem, wsem, xs_s, xs_r, c_s, c_r, g_s, g_r, i_s, i_r, e_s, e_r, w_s, w_r, f_s, f_r,
):
    group = lax.axis_index("groups")
    me = lax.axis_index("ep")
    mt = lax.axis_index("tp")
    QG = qs.shape[1] // KVH

    def dev(e, t):
        return (group, e, t)

    def remote(src, dst, ssem, rsem, e, t):
        return pltpu.make_async_remote_copy(
            src_ref=src, dst_ref=dst, send_sem=ssem, recv_sem=rsem,
            device_id=dev(e, t), device_id_type=MESH,
        )

    peers = [flip(mt, T - 1 - k) for k in range(T)]
    nexts = [lax.rem(me + j, N) for j in range(N)]

    load_x = pltpu.make_async_copy(x_hbm, xbuf.at[0], lsem.at[1])
    load_x.start()
    load_o = pltpu.make_async_copy(order_hbm, order_ref, lsem.at[6])
    load_o.start()
    load_kv = pltpu.make_async_copy(kv_hbm.at[0], kv_v, lsem.at[0])
    load_kv.start()
    load_l = pltpu.make_async_copy(len_hbm, len_ref, lsem.at[7])
    load_l.start()
    load_i = pltpu.make_async_copy(ids_hbm, ids_ref, lsem.at[8])
    load_i.start()
    load_s = pltpu.make_async_copy(rw_hbm, rw_ref, lsem.at[9])
    load_s.start()
    load_g = pltpu.make_async_copy(gain_hbm, gain_ref, lsem.at[10])
    load_g.start()
    load_w = []
    for k in range(T):
        cols = pl.ds(pl.multiple_of(peers[k] * FS, FS), FS)
        a = pltpu.make_async_copy(wg_hbm.at[0, :, cols], wg_v.at[k], wsem.at[0, k])
        b = pltpu.make_async_copy(wu_hbm.at[0, :, cols], wu_v.at[k], wsem.at[1, k])
        a.start()
        b.start()
        load_w.append((a, b))
    load_q = pltpu.make_async_copy(q_hbm, q_v, lsem.at[2])
    load_q.start()
    load_d = pltpu.make_async_copy(wd_hbm.at[0], wd_v, lsem.at[3])
    load_d.start()
    load_r = pltpu.make_async_copy(res_hbm, res_v, lsem.at[4])
    load_r.start()
    load_k = pltpu.make_async_copy(wkv_hbm, wkv_v, lsem.at[5])
    load_k.start()

    barrier = pltpu.get_barrier_semaphore()
    for j in range(N):
        for k in range(T):
            if j or k < T - 1:
                pl.semaphore_signal(
                    barrier, inc=1, device_id=dev(nexts[j], peers[k]), device_id_type=MESH
                )
    load_x.wait()
    pl.semaphore_wait(barrier, N * T - 1)

    dispatch, shares = [], []
    for j in range(1, N):
        c = remote(xbuf.at[0], xbuf.at[j], xs_s.at[j], xs_r.at[j], nexts[j], mt)
        c.start()
        dispatch.append(c)

    load_i.wait()
    load_s.wait()
    share = rw_ref[...] / jnp.sum(rw_ref[...], axis=0, keepdims=True)
    diagonal = lax.broadcasted_iota(jnp.int32, (R, R), 0) == lax.broadcasted_iota(
        jnp.int32, (R, R), 1
    )

    def weight_of(e):
        row = jnp.sum(jnp.where(ids_ref[...] == e, share, F32(0.0)), axis=0, keepdims=True)
        return jnp.sum(jnp.where(diagonal, row, F32(0.0)), axis=1, keepdims=True)

    for e in range(N):
        wsend[e] = jnp.broadcast_to(weight_of(e), (R, HD))
    for j in range(1, N):
        c = remote(wsend.at[nexts[j]], wrecv.at[j], w_s.at[j], w_r.at[j], nexts[j], mt)
        c.start()
        shares.append(c)

    def cache_copy(d, j):
        place = me * PJ + j
        t = place // M
        m = place % M
        i = d * PJ + j
        return (d == me) & (t == mt), m, remote(
            abuf.at[i], cbuf.at[mt, m], c_s.at[i], c_r.at[mt, m], d, t
        )

    load_o.wait()
    load_kv.wait()
    for d in range(N):
        for j in range(PJ):
            abuf[d * PJ + j] = kv_v[order_ref[0, d * PJ + j]]
            own, m, c = cache_copy(d, j)

            @pl.when(own)
            def _():
                cbuf[mt, m] = abuf[d * PJ + j]

            @pl.when(jnp.logical_not(own))
            def _():
                c.start()

    for c in dispatch:
        c.wait_recv()
    for e in range(N):
        slot = lax.rem(me - e + N, N)
        xs[e * R : (e + 1) * R, :] = xbuf[slot].astype(F32)
    x = xs[...].astype(BF16)

    scatter = []
    for k in range(T):
        load_w[k][0].wait()
        gate = jnp.dot(x, wg_v[k], preferred_element_type=F32)
        load_w[k][1].wait()
        up = jnp.dot(x, wu_v[k], preferred_element_type=F32)
        if k < T - 1:
            sbuf[k, :, :FS] = gate.astype(BF16)
            sbuf[k, :, FS:] = up.astype(BF16)
            c = remote(sbuf.at[k], rbuf.at[k], g_s.at[k], g_r.at[k], me, peers[k])
            c.start()
            scatter.append(c)
    load_q.wait()
    load_l.wait()
    load_g.wait()
    for m in range(M):
        for h in range(qs.shape[1]):
            qs[m, h : h + 1, :] = q_v[m : m + 1, h * HD : (h + 1) * HD].astype(F32)
    lane = lax.broadcasted_iota(jnp.int32, (1, HD), 1)
    half = jnp.where(lane < HD // 2, lane, lane - HD // 2).astype(F32)
    frequency = jnp.exp(half * F32(-2.0 / HD * math.log(1000000.0)))
    turns = []
    for m in range(M):
        angle = len_ref[m].astype(F32) * frequency
        sine = jnp.sin(angle)
        turns.append((jnp.cos(angle), jnp.where(lane < HD // 2, -sine, sine)))

    for k in range(T - 2, -1, -1):
        scatter[k].wait_recv()
        gate = gate + rbuf[k, :, :FS].astype(F32)
        up = up + rbuf[k, :, FS:].astype(F32)
    ibuf[T - 1] = (gate / (1.0 + jnp.exp(-gate)) * up).astype(BF16)
    gather = []
    for k in range(T - 1):
        c = remote(ibuf.at[T - 1], ibuf.at[k], i_s.at[k], i_r.at[k], me, peers[k])
        c.start()
        gather.append(c)

    load_r.wait()
    residual = res_v[...].astype(F32)
    for c in shares:
        c.wait_recv()
    for e in range(N):
        rp[e * R : (e + 1) * R, :] = jnp.where(me == e, residual, F32(0.0))
        slot = lax.rem(me - e + N, N)
        ws[e * R : (e + 1) * R, :] = jnp.where(me == e, wsend[me], wrecv[jnp.maximum(slot, 1)])
    load_d.wait()

    def down(k):
        rows = pl.ds(pl.multiple_of(peers[k] * FS, FS), FS)
        return jnp.dot(ibuf[k], wd_v[rows, :], preferred_element_type=F32)

    total = down(T - 1)
    for k in range(T - 2, -1, -1):
        gather[k].wait_recv()
        total = total + down(k)
    total = total.astype(BF16).astype(F32)
    rs[...] = total
    load_k.wait()
    terms = (rp[...] + ws[:, :1] * total).astype(BF16)
    total = jnp.dot(terms, wkv_v[...], preferred_element_type=F32)
    ps[...] = total
    for i in range(N * T):
        pbuf[i] = ps[i * M : (i + 1) * M, :]
    sums = []
    for j in range(N - 1, -1, -1):
        for k in range(T):
            if j or k < T - 1:
                i = j * T + k
                c = remote(
                    pbuf.at[nexts[j] * T + peers[k]], precv.at[i], f_s.at[i], f_r.at[i],
                    nexts[j], peers[k],
                )
                c.start()
                sums.append((i, c))
    for d in range(N):
        obuf[d] = rs[d * R : (d + 1) * R, :].astype(BF16)
    back = []
    for j in range(1, N):
        c = remote(obuf.at[nexts[j]], ebuf.at[j], e_s.at[j], e_r.at[j], nexts[j], mt)
        c.start()
        back.append(c)

    scale = F32(1.0 / math.sqrt(HD))
    parts = []
    for m in range(M):
        p = (mt * M + m) // PJ
        for t in range(T):
            @pl.when(jnp.logical_not((p == me) & (mt == t)))
            def _():
                remote(abuf.at[0], cbuf.at[t, m], c_s.at[0], c_r.at[t, m], p, t).wait_recv()
        live = lax.broadcasted_iota(jnp.int32, (QG, CTX), 1) < len_ref[m]
        for g in range(KVH):
            at = g * 2 * HD
            keys = cbuf[at // KF, m, :, at % KF : at % KF + HD]
            at = at + HD
            values = cbuf[at // KF, m, :, at % KF : at % KF + HD]
            query = qs[m, g * QG : (g + 1) * QG, :]
            scores = lax.dot_general(
                query.astype(BF16), keys, (((1,), (1,)), ((), ())), preferred_element_type=F32
            ) * scale
            scores = jnp.where(live, scores, F32(-1e30))
            top = jnp.max(scores, axis=1, keepdims=True)
            weights = jnp.where(live, jnp.exp(scores - top), F32(0.0))
            parts.append((
                query, top, jnp.sum(weights, axis=1, keepdims=True),
                jnp.dot(weights.astype(BF16), values, preferred_element_type=F32),
            ))

    mixed = res_v[...].astype(F32)
    for j in range(N):
        if j:
            back[j - 1].wait_recv()
        e = lax.rem(me - j + N, N)
        block = ebuf[j] if j else obuf[me]
        mixed = mixed + wsend[e][:, :1] * block.astype(F32)
    hid_ref[...] = mixed.astype(BF16)
    fresh = pbuf[me * T + mt]
    for i, c in sums:
        c.wait_recv()
    for i, c in sums:
        fresh = fresh + precv[i]
    fresh = fresh.astype(BF16).astype(F32)

    for m in range(M):
        cosine, sine = turns[m]
        for g in range(KVH):
            at = g * 2 * HD
            key = fresh[m : m + 1, at : at + HD]
            value = fresh[m : m + 1, at + HD : at + 2 * HD]
            factor = lax.rsqrt(jnp.mean(key * key, axis=1, keepdims=True) + F32(1e-6))
            key = key * factor * gain_ref[...]
            key = (key * cosine + pltpu.roll(key, HD // 2, 1) * sine).astype(BF16).astype(F32)
            query, top, weight, summed = parts[m * KVH + g]
            score = jnp.sum(query * key, axis=1, keepdims=True) * scale
            most = jnp.maximum(top, score)
            old = jnp.exp(top - most)
            new = jnp.exp(score - most)
            out = (summed * old + new * value) / (weight * old + new)
            att_ref[m, g * QG : (g + 1) * QG, :] = out.astype(BF16)

    for c in dispatch + shares + scatter + gather + back + [c for _, c in sums]:
        c.wait_send()
    for d in range(N):
        for j in range(PJ):
            own, m, c = cache_copy(d, j)

            @pl.when(jnp.logical_not(own))
            def _():
                c.wait_send()


def on_device(
    normed, residual, expert_ids, route_weight, w_gate, w_up, w_down, w_kv,
    key_gain, prefill_kv, order, lengths, queries,
):
    N = lax.axis_size("ep")
    T = lax.axis_size("tp")
    R, W = normed.shape
    M = lengths.shape[0]
    _, requests, CTX, KF = prefill_kv.shape
    PJ = requests // N
    FF = w_gate.shape[2]
    FS = FF // T
    KVF = w_kv.shape[1]
    heads = queries.shape[1] // HD
    rows = N * R
    choices = expert_ids.shape[1]
    dma = pltpu.SemaphoreType.DMA
    hbm = pl.BlockSpec(memory_space=pltpu.HBM)
    vmem = pl.BlockSpec(memory_space=pltpu.VMEM)
    hidden_state, attention = pl.pallas_call(
        functools.partial(kernel, N, T, R, M, PJ, CTX, KF, FS),
        out_shape=(
            jax.ShapeDtypeStruct((R, W), BF16),
            jax.ShapeDtypeStruct((M, heads, HD), BF16),
        ),
        in_specs=[hbm] * 13,
        out_specs=(vmem, vmem),
        scratch_shapes=[
            pltpu.VMEM((choices, R), jnp.int32),
            pltpu.VMEM((choices, R), F32),
            pltpu.VMEM((1, HD), F32),
            pltpu.SMEM((1, requests), jnp.int32),
            pltpu.SMEM((M,), jnp.int32),
            pltpu.VMEM((N, R, W), BF16),
            pltpu.VMEM((rows, W), F32),
            pltpu.VMEM((T, W, FS), BF16),
            pltpu.VMEM((T, W, FS), BF16),
            pltpu.VMEM((FF, W), BF16),
            pltpu.VMEM((W, KVF), BF16),
            pltpu.VMEM((R, W), BF16),
            pltpu.VMEM((M, heads * HD), BF16),
            pltpu.VMEM((M, heads, HD), F32),
            pltpu.VMEM((requests, CTX, KF), BF16),
            pltpu.VMEM((requests, CTX, KF), BF16),
            pltpu.VMEM((T, M, CTX, KF), BF16),
            pltpu.VMEM((T - 1, rows, 2 * FS), BF16),
            pltpu.VMEM((T - 1, rows, 2 * FS), BF16),
            pltpu.VMEM((T, rows, FS), BF16),
            pltpu.VMEM((rows, W), F32),
            pltpu.VMEM((N, R, W), BF16),
            pltpu.VMEM((N, R, W), BF16),
            pltpu.VMEM((N, R, HD), F32),
            pltpu.VMEM((N, R, HD), F32),
            pltpu.VMEM((rows, HD), F32),
            pltpu.VMEM((rows, W), F32),
            pltpu.VMEM((rows, KVF), F32),
            pltpu.VMEM((N * T, M, KVF), F32),
            pltpu.VMEM((N * T, M, KVF), F32),
            dma((11,)), dma((2, T)),
            dma((N,)), dma((N,)),
            dma((requests,)), dma((T, M)),
            dma((T - 1,)), dma((T - 1,)),
            dma((T - 1,)), dma((T - 1,)),
            dma((N,)), dma((N,)),
            dma((N,)), dma((N,)),
            dma((N * T,)), dma((N * T,)),
        ],
        compiler_params=pltpu.CompilerParams(
            collective_id=0, has_side_effects=True, vmem_limit_bytes=48 * 1024 * 1024
        ),
    )(
        *[
            pltpu.with_memory_space_constraint(value, pltpu.HBM)
            for value in (
                normed, residual, expert_ids.T, route_weight.T, w_gate, w_up, w_down, w_kv,
                key_gain.reshape(1, HD), prefill_kv, order,
            )
        ],
        lengths,
        pltpu.with_memory_space_constraint(queries, pltpu.HBM),
    )
    return hidden_state, attention.reshape(M, heads * HD)


def solution(mesh):
    in_specs = (
        P(("groups", "ep"), "tp"),
        P(("groups", "ep"), "tp"),
        P(("groups", "ep"), None),
        P(("groups", "ep"), None),
        P("ep", "tp", None),
        P("ep", "tp", None),
        P("ep", None, "tp"),
        P("tp", None),
        P(),
        P(("groups", "ep"), None, None, "tp"),
        P(("groups", "ep"), None),
        P(("groups", "ep", "tp")),
        P(("groups", "ep", "tp"), None),
    )
    out_specs = (P(("groups", "ep"), "tp"), P(("groups", "ep", "tp"), None))
    return jax.shard_map(
        on_device, mesh=mesh, in_specs=in_specs, out_specs=out_specs, check_vma=False
    )
```

```python
import functools
import math

import jax
import jax.numpy as jnp
from jax import lax
from jax.experimental import pallas as pl
from jax.experimental.pallas import tpu as pltpu
from jax.sharding import PartitionSpec as P

KVH = 4
HD = 128
MESH = pl.DeviceIdType.MESH
F32 = jnp.float32
BF16 = jnp.bfloat16


def flip(index, mask):
    out = index
    bit = 1
    while bit <= mask:
        if mask & bit:
            out = out + bit - 2 * bit * ((index // bit) % 2)
        bit *= 2
    return out


def kernel(
    N, T, R, M, PJ, CTX, KF, FS,
    x_hbm, res_hbm, ids_hbm, rw_hbm, wg_hbm, wu_hbm, wd_hbm, wkv_hbm, gain_hbm,
    kv_hbm, order_hbm, len_hbm, q_hbm,
    hid_ref, att_ref,
    ids_ref, rw_ref, gain_ref, order_ref, len_ref,
    xbuf, xs, wg_v, wu_v, wd_v, wkv_v, res_v, q_v, qs, kv_v, abuf, cbuf,
    sbuf, rbuf, ibuf, rs, obuf, ebuf, wsend, wrecv, ws, rp, ps, pbuf, precv,
    lsem, wsem, xs_s, xs_r, c_s, c_r, g_s, g_r, i_s, i_r, e_s, e_r, w_s, w_r, f_s, f_r,
):
    group = lax.axis_index("groups")
    me = lax.axis_index("ep")
    mt = lax.axis_index("tp")
    QG = qs.shape[1] // KVH

    def dev(e, t):
        return (group, e, t)

    def remote(src, dst, ssem, rsem, e, t):
        return pltpu.make_async_remote_copy(
            src_ref=src, dst_ref=dst, send_sem=ssem, recv_sem=rsem,
            device_id=dev(e, t), device_id_type=MESH,
        )

    peers = [flip(mt, T - 1 - k) for k in range(T)]
    nexts = [lax.rem(me + j, N) for j in range(N)]

    load_x = pltpu.make_async_copy(x_hbm, xbuf.at[0], lsem.at[1])
    load_x.start()
    load_o = pltpu.make_async_copy(order_hbm, order_ref, lsem.at[6])
    load_o.start()
    load_kv = pltpu.make_async_copy(kv_hbm.at[0], kv_v, lsem.at[0])
    load_kv.start()
    load_l = pltpu.make_async_copy(len_hbm, len_ref, lsem.at[7])
    load_l.start()
    load_i = pltpu.make_async_copy(ids_hbm, ids_ref, lsem.at[8])
    load_i.start()
    load_s = pltpu.make_async_copy(rw_hbm, rw_ref, lsem.at[9])
    load_s.start()
    load_g = pltpu.make_async_copy(gain_hbm, gain_ref, lsem.at[10])
    load_g.start()
    load_w = []
    for k in range(T):
        cols = pl.ds(pl.multiple_of(peers[k] * FS, FS), FS)
        a = pltpu.make_async_copy(wg_hbm.at[0, :, cols], wg_v.at[k], wsem.at[0, k])
        b = pltpu.make_async_copy(wu_hbm.at[0, :, cols], wu_v.at[k], wsem.at[1, k])
        a.start()
        b.start()
        load_w.append((a, b))
    load_q = pltpu.make_async_copy(q_hbm, q_v, lsem.at[2])
    load_q.start()
    load_d = pltpu.make_async_copy(wd_hbm.at[0], wd_v, lsem.at[3])
    load_d.start()
    load_r = pltpu.make_async_copy(res_hbm, res_v, lsem.at[4])
    load_r.start()
    load_k = pltpu.make_async_copy(wkv_hbm, wkv_v, lsem.at[5])
    load_k.start()

    barrier = pltpu.get_barrier_semaphore()
    for j in range(N):
        for k in range(T):
            if j or k < T - 1:
                pl.semaphore_signal(
                    barrier, inc=1, device_id=dev(nexts[j], peers[k]), device_id_type=MESH
                )
    load_i.wait()
    load_s.wait()
    share = rw_ref[...] / jnp.sum(rw_ref[...], axis=0, keepdims=True)
    diagonal = lax.broadcasted_iota(jnp.int32, (R, R), 0) == lax.broadcasted_iota(
        jnp.int32, (R, R), 1
    )

    def weight_of(e):
        row = jnp.sum(jnp.where(ids_ref[...] == e, share, F32(0.0)), axis=0, keepdims=True)
        return jnp.sum(jnp.where(diagonal, row, F32(0.0)), axis=1, keepdims=True)

    for e in range(N):
        wsend[e] = jnp.broadcast_to(weight_of(e), (R, HD))
    load_x.wait()
    pl.semaphore_wait(barrier, N * T - 1)

    dispatch, shares = [], []
    for j in range(1, N):
        c = remote(xbuf.at[0], xbuf.at[j], xs_s.at[j], xs_r.at[j], nexts[j], mt)
        c.start()
        dispatch.append(c)

    for j in range(1, N):
        c = remote(wsend.at[nexts[j]], wrecv.at[j], w_s.at[j], w_r.at[j], nexts[j], mt)
        c.start()
        shares.append(c)

    def cache_copy(d, j):
        place = me * PJ + j
        t = place // M
        m = place % M
        i = d * PJ + j
        return (d == me) & (t == mt), m, remote(
            abuf.at[i], cbuf.at[mt, m], c_s.at[i], c_r.at[mt, m], d, t
        )

    load_o.wait()
    load_kv.wait()
    for d in range(N):
        for j in range(PJ):
            abuf[d * PJ + j] = kv_v[order_ref[0, d * PJ + j]]
            own, m, c = cache_copy(d, j)

            @pl.when(own)
            def _():
                cbuf[mt, m] = abuf[d * PJ + j]

            @pl.when(jnp.logical_not(own))
            def _():
                c.start()

    for c in dispatch:
        c.wait_recv()
    for e in range(N):
        slot = lax.rem(me - e + N, N)
        xs[e * R : (e + 1) * R, :] = xbuf[slot].astype(F32)
    x = xs[...].astype(BF16)

    scatter = []
    for k in range(T):
        load_w[k][0].wait()
        gate = jnp.dot(x, wg_v[k], preferred_element_type=F32)
        load_w[k][1].wait()
        up = jnp.dot(x, wu_v[k], preferred_element_type=F32)
        if k < T - 1:
            sbuf[k, :, :FS] = gate.astype(BF16)
            sbuf[k, :, FS:] = up.astype(BF16)
            c = remote(sbuf.at[k], rbuf.at[k], g_s.at[k], g_r.at[k], me, peers[k])
            c.start()
            scatter.append(c)
    load_q.wait()
    load_l.wait()
    load_g.wait()
    for m in range(M):
        for h in range(qs.shape[1]):
            qs[m, h : h + 1, :] = q_v[m : m + 1, h * HD : (h + 1) * HD].astype(F32)
    lane = lax.broadcasted_iota(jnp.int32, (1, HD), 1)
    half = jnp.where(lane < HD // 2, lane, lane - HD // 2).astype(F32)
    frequency = jnp.exp(half * F32(-2.0 / HD * math.log(1000000.0)))
    turns = []
    for m in range(M):
        angle = len_ref[m].astype(F32) * frequency
        sine = jnp.sin(angle)
        turns.append((jnp.cos(angle), jnp.where(lane < HD // 2, -sine, sine)))

    for k in range(T - 2, -1, -1):
        scatter[k].wait_recv()
        gate = gate + rbuf[k, :, :FS].astype(F32)
        up = up + rbuf[k, :, FS:].astype(F32)
    ibuf[T - 1] = (gate / (1.0 + jnp.exp(-gate)) * up).astype(BF16)
    gather = []
    for k in range(T - 1):
        c = remote(ibuf.at[T - 1], ibuf.at[k], i_s.at[k], i_r.at[k], me, peers[k])
        c.start()
        gather.append(c)

    load_r.wait()
    residual = res_v[...].astype(F32)
    for c in shares:
        c.wait_recv()
    for e in range(N):
        rp[e * R : (e + 1) * R, :] = jnp.where(me == e, residual, F32(0.0))
        slot = lax.rem(me - e + N, N)
        ws[e * R : (e + 1) * R, :] = jnp.where(me == e, wsend[me], wrecv[jnp.maximum(slot, 1)])
    load_d.wait()

    def down(k):
        rows = pl.ds(pl.multiple_of(peers[k] * FS, FS), FS)
        return jnp.dot(ibuf[k], wd_v[rows, :], preferred_element_type=F32)

    total = down(T - 1)
    for k in range(T - 2, -1, -1):
        gather[k].wait_recv()
        total = total + down(k)
    total = total.astype(BF16).astype(F32)
    rs[...] = total
    load_k.wait()
    terms = (rp[...] + ws[:, :1] * total).astype(BF16)
    total = jnp.dot(terms, wkv_v[...], preferred_element_type=F32)
    ps[...] = total
    for i in range(N * T):
        pbuf[i] = ps[i * M : (i + 1) * M, :]
    sums = []
    for j in range(N - 1, -1, -1):
        for k in range(T):
            if j or k < T - 1:
                i = j * T + k
                c = remote(
                    pbuf.at[nexts[j] * T + peers[k]], precv.at[i], f_s.at[i], f_r.at[i],
                    nexts[j], peers[k],
                )
                c.start()
                sums.append((i, c))
    for d in range(N):
        obuf[d] = rs[d * R : (d + 1) * R, :].astype(BF16)
    back = []
    for j in range(1, N):
        c = remote(obuf.at[nexts[j]], ebuf.at[j], e_s.at[j], e_r.at[j], nexts[j], mt)
        c.start()
        back.append(c)

    scale = F32(1.0 / math.sqrt(HD))
    parts = []
    for m in range(M):
        p = (mt * M + m) // PJ
        for t in range(T):
            @pl.when(jnp.logical_not((p == me) & (mt == t)))
            def _():
                remote(abuf.at[0], cbuf.at[t, m], c_s.at[0], c_r.at[t, m], p, t).wait_recv()
        live = lax.broadcasted_iota(jnp.int32, (QG, CTX), 1) < len_ref[m]
        for g in range(KVH):
            at = g * 2 * HD
            keys = cbuf[at // KF, m, :, at % KF : at % KF + HD]
            at = at + HD
            values = cbuf[at // KF, m, :, at % KF : at % KF + HD]
            query = qs[m, g * QG : (g + 1) * QG, :]
            scores = lax.dot_general(
                query.astype(BF16), keys, (((1,), (1,)), ((), ())), preferred_element_type=F32
            ) * scale
            scores = jnp.where(live, scores, F32(-1e30))
            top = jnp.max(scores, axis=1, keepdims=True)
            weights = jnp.where(live, jnp.exp(scores - top), F32(0.0))
            parts.append((
                query, top, jnp.sum(weights, axis=1, keepdims=True),
                jnp.dot(weights.astype(BF16), values, preferred_element_type=F32),
            ))

    mixed = res_v[...].astype(F32)
    for j in range(N):
        if j:
            back[j - 1].wait_recv()
        e = lax.rem(me - j + N, N)
        block = ebuf[j] if j else obuf[me]
        mixed = mixed + wsend[e][:, :1] * block.astype(F32)
    hid_ref[...] = mixed.astype(BF16)
    fresh = pbuf[me * T + mt]
    for i, c in sums:
        c.wait_recv()
    for i, c in sums:
        fresh = fresh + precv[i]
    fresh = fresh.astype(BF16).astype(F32)

    for m in range(M):
        cosine, sine = turns[m]
        for g in range(KVH):
            at = g * 2 * HD
            key = fresh[m : m + 1, at : at + HD]
            value = fresh[m : m + 1, at + HD : at + 2 * HD]
            factor = lax.rsqrt(jnp.mean(key * key, axis=1, keepdims=True) + F32(1e-6))
            key = key * factor * gain_ref[...]
            key = (key * cosine + pltpu.roll(key, HD // 2, 1) * sine).astype(BF16).astype(F32)
            query, top, weight, summed = parts[m * KVH + g]
            score = jnp.sum(query * key, axis=1, keepdims=True) * scale
            most = jnp.maximum(top, score)
            old = jnp.exp(top - most)
            new = jnp.exp(score - most)
            out = (summed * old + new * value) / (weight * old + new)
            att_ref[m, g * QG : (g + 1) * QG, :] = out.astype(BF16)

    for c in dispatch + shares + scatter + gather + back + [c for _, c in sums]:
        c.wait_send()
    for d in range(N):
        for j in range(PJ):
            own, m, c = cache_copy(d, j)

            @pl.when(jnp.logical_not(own))
            def _():
                c.wait_send()


def on_device(
    normed, residual, expert_ids, route_weight, w_gate, w_up, w_down, w_kv,
    key_gain, prefill_kv, order, lengths, queries,
):
    N = lax.axis_size("ep")
    T = lax.axis_size("tp")
    R, W = normed.shape
    M = lengths.shape[0]
    _, requests, CTX, KF = prefill_kv.shape
    PJ = requests // N
    FF = w_gate.shape[2]
    FS = FF // T
    KVF = w_kv.shape[1]
    heads = queries.shape[1] // HD
    rows = N * R
    choices = expert_ids.shape[1]
    dma = pltpu.SemaphoreType.DMA
    hbm = pl.BlockSpec(memory_space=pltpu.HBM)
    vmem = pl.BlockSpec(memory_space=pltpu.VMEM)
    hidden_state, attention = pl.pallas_call(
        functools.partial(kernel, N, T, R, M, PJ, CTX, KF, FS),
        out_shape=(
            jax.ShapeDtypeStruct((R, W), BF16),
            jax.ShapeDtypeStruct((M, heads, HD), BF16),
        ),
        in_specs=[hbm] * 13,
        out_specs=(vmem, vmem),
        scratch_shapes=[
            pltpu.VMEM((choices, R), jnp.int32),
            pltpu.VMEM((choices, R), F32),
            pltpu.VMEM((1, HD), F32),
            pltpu.SMEM((1, requests), jnp.int32),
            pltpu.SMEM((M,), jnp.int32),
            pltpu.VMEM((N, R, W), BF16),
            pltpu.VMEM((rows, W), F32),
            pltpu.VMEM((T, W, FS), BF16),
            pltpu.VMEM((T, W, FS), BF16),
            pltpu.VMEM((FF, W), BF16),
            pltpu.VMEM((W, KVF), BF16),
            pltpu.VMEM((R, W), BF16),
            pltpu.VMEM((M, heads * HD), BF16),
            pltpu.VMEM((M, heads, HD), F32),
            pltpu.VMEM((requests, CTX, KF), BF16),
            pltpu.VMEM((requests, CTX, KF), BF16),
            pltpu.VMEM((T, M, CTX, KF), BF16),
            pltpu.VMEM((T - 1, rows, 2 * FS), BF16),
            pltpu.VMEM((T - 1, rows, 2 * FS), BF16),
            pltpu.VMEM((T, rows, FS), BF16),
            pltpu.VMEM((rows, W), F32),
            pltpu.VMEM((N, R, W), BF16),
            pltpu.VMEM((N, R, W), BF16),
            pltpu.VMEM((N, R, HD), F32),
            pltpu.VMEM((N, R, HD), F32),
            pltpu.VMEM((rows, HD), F32),
            pltpu.VMEM((rows, W), F32),
            pltpu.VMEM((rows, KVF), F32),
            pltpu.VMEM((N * T, M, KVF), F32),
            pltpu.VMEM((N * T, M, KVF), F32),
            dma((11,)), dma((2, T)),
            dma((N,)), dma((N,)),
            dma((requests,)), dma((T, M)),
            dma((T - 1,)), dma((T - 1,)),
            dma((T - 1,)), dma((T - 1,)),
            dma((N,)), dma((N,)),
            dma((N,)), dma((N,)),
            dma((N * T,)), dma((N * T,)),
        ],
        compiler_params=pltpu.CompilerParams(
            collective_id=0, has_side_effects=True, vmem_limit_bytes=48 * 1024 * 1024
        ),
    )(
        *[
            pltpu.with_memory_space_constraint(value, pltpu.HBM)
            for value in (
                normed, residual, expert_ids.T, route_weight.T, w_gate, w_up, w_down, w_kv,
                key_gain.reshape(1, HD), prefill_kv, order,
            )
        ],
        lengths,
        pltpu.with_memory_space_constraint(queries, pltpu.HBM),
    )
    return hidden_state, attention.reshape(M, heads * HD)


def solution(mesh):
    in_specs = (
        P(("groups", "ep"), "tp"),
        P(("groups", "ep"), "tp"),
        P(("groups", "ep"), None),
        P(("groups", "ep"), None),
        P("ep", "tp", None),
        P("ep", "tp", None),
        P("ep", None, "tp"),
        P("tp", None),
        P(),
        P(("groups", "ep"), None, None, "tp"),
        P(("groups", "ep"), None),
        P(("groups", "ep", "tp")),
        P(("groups", "ep", "tp"), None),
    )
    out_specs = (P(("groups", "ep"), "tp"), P(("groups", "ep", "tp"), None))
    return jax.shard_map(
        on_device, mesh=mesh, in_specs=in_specs, out_specs=out_specs, check_vma=False
    )
```
